32 devices in a mesh: dp: 4 (over y, x), entity: 8 (over z, core).
Axes of the slice: x: 2, y: 2, z: 4, core: 2. Of those that a mesh axis runs over, the one named last changes fastest.
Arguments:
- entities: float32 [8, 4096, 256], P('entity'), may hold values from -20 to 20
- relations: float32 [256, 256, 256], P('entity'), may hold values from -0.375 to 0.375
- candidate_blocks: int32 [32, 8], P('dp'), may hold values from 0 to 7, as said below
- list_lengths: int32 [4, 8], P('dp'), may hold values from 2 to 8, as said below
- head_offsets: int32 [4096], P(('dp', 'entity')), may hold values from 0 to 4095
- relation_offsets: int32 [4096], P(('dp', 'entity')), may hold values from 0 to 31
- target_codes: int32 [4096], P(('dp', 'entity')), may hold values from 0 to 32767
Outputs:
- loss: float32 [4096], P(('dp', 'entity'))
- entity_grad: float32 [8, 4096, 256], P('entity', 'dp')
The draws below stay inside these ranges and needn't reach their ends.
Inputs may be any that keep to these rules, and one draw needn't show every extreme that they name: `candidate_blocks`: each row names 8 different blocks. Among the entries of the 8 rows of one dp group, used or not, no block is named more than 8 times; in every dp group one block is named exactly 8 times, each time at a used entry. `list_lengths`: the 8 lengths of one dp group sum to 40, and one of them is 8.
All inputs are finite; a program needn't handle non-finite values.
Results may differ from the reference program's by a relative error of at most 0.0025.
The reference program's roundings to bfloat16 on the way count: a program that leaves them out, or rounds other values in their place, can miss the bound.
Values may be sent and summed in bfloat16 or wider, within the bound.
A program may use at most 64 MiB of HBM per device.

```python
import jax
import jax.numpy as jnp
from jax import lax

D = 256
RELS = 256
BLOCK = 4096
TOP = 8
TRIP_DEV = 128
NBLOCKS = 8
REL_DEV = 32
SETS = 32
TRIPLES = 4096
MOST = 8
N_DP = 4
N_ENTITY = 8


def draw_entities(key, part):
    first, second = jax.random.split(key, 2)
    base = jnp.clip(jax.random.normal(first, (NBLOCKS, BLOCK, D), jnp.float32), -6.0, 6.0)
    scales = jnp.exp(jax.random.uniform(second, (NBLOCKS, BLOCK, 1), jnp.float32, -0.4, 0.4))
    values = 0.35 * base * scales
    return values


def draw_lists(key):
    group_total = SETS // NBLOCKS
    row_total = NBLOCKS
    half_total = row_total // 2

    def one_group(group_key):
        order_key, shuffle_key, row_key, length_key, place_key = jax.random.split(group_key, 5)
        block_order = jax.random.permutation(order_key, row_total).astype(jnp.int32)
        row_index = jnp.arange(row_total, dtype=jnp.int32)
        column = jnp.arange(TOP, dtype=jnp.int32)
        position = (row_index[:, None] + column[None, :]) % row_total
        holds = position == 0
        contains = jnp.any(holds, axis=1)
        extra = (row_index >= 1) & (row_index <= MOST - TOP)
        crowded = contains | extra
        leading = position[:, :1]
        swapped = jnp.where(holds, leading, position)
        lead_column = (column[None, :] == 0) & crowded[:, None]
        placed = jnp.where(lead_column, 0, swapped)
        scores = jax.random.randint(shuffle_key, (row_total, TOP), 0, 1024, dtype=jnp.int32) * TOP + column[None, :]
        scores = jnp.where(lead_column, -1, scores)
        ordering = jnp.argsort(scores, axis=1, stable=True)
        shuffled = jnp.take_along_axis(placed, ordering, axis=1)
        named = jnp.take(block_order, shuffled)
        row_order = jax.random.permutation(row_key, row_total)
        named = jnp.take(named, row_order, axis=0)
        firsts = jax.random.randint(length_key, (half_total,), 2, TOP + 1, dtype=jnp.int32)
        firsts = jnp.where(jnp.arange(half_total, dtype=jnp.int32) == 0, TOP, firsts)
        paired = jnp.stack([firsts, 10 - firsts], axis=1).reshape(row_total)
        length_order = jax.random.permutation(place_key, row_total)
        return (named.astype(jnp.int32), jnp.take(paired, length_order).astype(jnp.int32))
    named, lengths = jax.vmap(one_group)(jax.random.split(key, group_total))
    return (named.reshape(group_total * row_total, TOP), lengths)


def draw_candidate_blocks(key, part):
    return draw_lists(jax.random.fold_in(key, 7))[0]


def draw_list_lengths(key, part):
    return draw_lists(jax.random.fold_in(key, 7))[1]


def set_ends(entries, rng, smallest, top_value):
    extent = entries.shape
    index_at = [jax.random.randint(jax.random.fold_in(rng, axis), (), 0, extent[axis]) for axis in range(len(extent))]
    entries = entries.at[tuple(index_at)].set(smallest)
    longest = extent.index(max(extent))
    index_at[longest] = (index_at[longest] + 1) % extent[longest]
    return entries.at[tuple(index_at)].set(top_value)


def level_of(rng, shape, shards, least, largest):
    loudness, own = 1.0, jax.random.fold_in(rng, 6)
    for axis_at, parts in shards:
        steps = jnp.exp(jax.random.uniform(jax.random.fold_in(own, axis_at), (parts,), jnp.float32, least / len(shards), largest / len(shards)))
        loudness = loudness * jnp.repeat(steps, shape[axis_at] // parts).reshape([-1 if axis == axis_at else 1 for axis in range(len(shape))])
    return loudness


def centred(key, extent, spread, bound, shards=(), held_as=jnp.bfloat16):
    result = jax.random.normal(key, extent, jnp.float32) * spread
    if len(shards) > 0:
        result = level_of(key, extent, shards, -0.22, 0.18) * result
    return jnp.clip(result, min=-bound, max=bound).astype(held_as)


def setup_inputs(seed: int = 0) -> dict:
    key_of = jax.random.split(jax.random.key(seed), 8)
    return {
        "entities": draw_entities(jax.random.fold_in(key_of[7], 71), 0),
        "relations": centred(key_of[1], (RELS, D, D), D ** -0.5, 0.375, ((0, 8),), jnp.float32),
        "candidate_blocks": draw_candidate_blocks(jax.random.fold_in(key_of[7], 71), 0),
        "list_lengths": draw_list_lengths(jax.random.fold_in(key_of[7], 71), 0),
        "head_offsets": set_ends(jax.random.randint(key_of[4], (TRIPLES,), 0, BLOCK), jax.random.fold_in(key_of[4], 1), 0, BLOCK - 1).astype(jnp.int32),
        "relation_offsets": set_ends(jax.random.randint(key_of[5], (TRIPLES,), 0, REL_DEV), jax.random.fold_in(key_of[5], 1), 0, REL_DEV - 1).astype(jnp.int32),
        "target_codes": set_ends(jax.random.randint(key_of[6], (TRIPLES,), 0, TOP * BLOCK), jax.random.fold_in(key_of[6], 1), 0, (TOP * BLOCK) - 1).astype(jnp.int32),
    }


negative_floor = -1e30


def combine_stats(earlier, latter):
    first_max, first_sum, first_target = earlier
    second_max, second_sum, second_target = latter
    larger = jnp.maximum(first_max, second_max)
    combined = first_sum * jnp.exp(first_max - larger) + second_sum * jnp.exp(second_max - larger)
    return (larger, combined, first_target + second_target)


def keep_value(current):
    return current


def reference(entities, relations, candidate_blocks, list_lengths, head_offsets, relation_offsets, target_codes):
    set_total = N_DP * N_ENTITY
    local_relations = RELS // N_ENTITY
    lengths = list_lengths.reshape(set_total)
    head_grid = head_offsets.reshape(set_total, TRIP_DEV)
    kind_grid = relation_offsets.reshape(set_total, TRIP_DEV)
    code_grid = target_codes.reshape(set_total, TRIP_DEV)
    rounded = lax.optimization_barrier(entities.astype(jnp.bfloat16))

    def make_query(set_number):
        home = set_number % N_ENTITY
        table = lax.dynamic_index_in_dim(entities, home, 0, keepdims=False)
        head_rows = jnp.take(table, head_grid[set_number], axis=0)
        chosen = lax.dynamic_slice_in_dim(relations, home * local_relations, local_relations, 0)
        products = jnp.einsum("td,rde->tre", head_rows, chosen, precision=lax.Precision.HIGHEST)
        selector = (kind_grid[set_number][:, None] == jnp.arange(local_relations, dtype=jnp.int32)[None, :]).astype(jnp.float32)
        return jnp.sum(products * selector[:, :, None], axis=1).astype(jnp.bfloat16)

    queries = lax.map(make_query, jnp.arange(set_total, dtype=jnp.int32))
    picks = ((code_grid // BLOCK) % lengths[:, None]).astype(jnp.int32)
    target_block = jnp.take_along_axis(candidate_blocks, picks, axis=1)
    target_row = (code_grid % BLOCK).astype(jnp.int32)
    positions = jnp.arange(BLOCK, dtype=jnp.int32)

    def block_scores(query_full, block):
        keys = lax.dynamic_index_in_dim(rounded, block, 0, keepdims=False).astype(jnp.float32)
        return jnp.dot(query_full, keys.T, precision=lax.Precision.HIGHEST)

    def target_mask(set_number, block):
        same_block = target_block[set_number][:, None] == block
        return same_block & (positions[None, :] == target_row[set_number][:, None])

    def set_stats(set_number):
        query_full = queries[set_number].astype(jnp.float32)

        def visit(carry, entry):
            def include(current):
                block = candidate_blocks[set_number, entry]
                scores = block_scores(query_full, block)
                maxima = jnp.max(scores, axis=1)
                masses = jnp.sum(jnp.exp(scores - maxima[:, None]), axis=1)
                picked = jnp.sum(jnp.where(target_mask(set_number, block), scores, 0.0), axis=1)
                return combine_stats(current, (maxima, masses, picked))
            return lax.cond(entry < lengths[set_number], include, keep_value, carry), None

        initial = (jnp.full((TRIP_DEV,), negative_floor, jnp.float32), jnp.zeros((TRIP_DEV,), jnp.float32), jnp.zeros((TRIP_DEV,), jnp.float32))
        final, unused = lax.scan(visit, initial, jnp.arange(TOP, dtype=jnp.int32))
        return final

    maxima, masses, picked = lax.map(set_stats, jnp.arange(set_total, dtype=jnp.int32))
    log_norm = maxima + jnp.log(masses)
    loss = (log_norm - picked).reshape(-1)

    def set_grads(gradient, set_number):
        query_full = queries[set_number].astype(jnp.float32)
        norm_row = log_norm[set_number]

        def visit(current, entry):
            block = candidate_blocks[set_number, entry]

            def include(unused_value):
                scores = block_scores(query_full, block)
                weights = jnp.exp(scores - norm_row[:, None])
                coefficients = (weights - target_mask(set_number, block).astype(jnp.float32)).astype(jnp.bfloat16)
                coefficients = lax.optimization_barrier(coefficients).astype(jnp.float32)
                return jnp.dot(coefficients.T, query_full, precision=lax.Precision.HIGHEST)

            def nothing(unused_value):
                return jnp.zeros((BLOCK, D), jnp.float32)

            update = lax.cond(entry < lengths[set_number], include, nothing, 0)
            previous = lax.dynamic_index_in_dim(current, block, 0, keepdims=False)
            return lax.dynamic_update_index_in_dim(current, previous + update, block, 0), None

        gradient, unused = lax.scan(visit, gradient, jnp.arange(TOP, dtype=jnp.int32))
        return gradient, None

    gradient, unused = lax.scan(set_grads, jnp.zeros((NBLOCKS, BLOCK, D), jnp.float32), jnp.arange(set_total, dtype=jnp.int32))
    return (loss, gradient)
```

```python
import jax
import jax.numpy as jnp
from jax import lax
from jax.experimental import pallas as pl
from jax.experimental.pallas import tpu as pltpu
from jax.sharding import PartitionSpec as P

CAP = 12


negative_floor = -1e30
slots_per_step = 4


def score_rows(queries, row_block):
    return lax.dot_general(
        queries, row_block, (((1,), (1,)), ((), ())), preferred_element_type=jnp.float32
    )


def step_view(values, slot_count):
    return values.reshape(
        (slot_count // slots_per_step, slots_per_step * values.shape[1]) + values.shape[2:]
    )


def slot_stats(row_block, queries, targets, in_use):
    slot_count, trip_count = targets.shape
    active = jnp.broadcast_to(in_use[:, None], (slot_count, trip_count))
    positions = jnp.arange(row_block.shape[0], dtype=jnp.int32)

    def one_step(inputs):
        step_queries, step_targets = inputs
        scores = score_rows(step_queries, row_block)
        maxima = jnp.max(scores, axis=1)
        masses = jnp.sum(jnp.exp(scores - maxima[:, None]), axis=1)
        is_target = positions[None, :] == step_targets[:, None]
        picked = jnp.sum(jnp.where(is_target, scores, 0.0), axis=1)
        return (maxima, masses, picked)

    maxima, masses, picked = lax.map(
        one_step, (step_view(queries, slot_count), step_view(targets, slot_count))
    )
    maxima = jnp.where(active, maxima.reshape(slot_count, trip_count), negative_floor)
    masses = jnp.where(active, masses.reshape(slot_count, trip_count), 0.0)
    picked = jnp.where(active, picked.reshape(slot_count, trip_count), 0.0)
    return (maxima, masses, picked)


def slot_grads(row_block, queries, targets, in_use, slot_norms):
    slot_count, trip_count = targets.shape
    active = jnp.broadcast_to(in_use[:, None], (slot_count, trip_count))
    positions = jnp.arange(row_block.shape[0], dtype=jnp.int32)

    def one_step(carry, inputs):
        step_queries, step_targets, step_norms, step_active = inputs
        scores = score_rows(step_queries, row_block)
        weights = jnp.exp(scores - step_norms[:, None])
        is_target = (positions[None, :] == step_targets[:, None]).astype(jnp.float32)
        coefficients = jnp.where(step_active[:, None], weights - is_target, 0.0).astype(
            jnp.bfloat16
        )
        update = lax.dot_general(
            coefficients, step_queries, (((0,), (0,)), ((), ())), preferred_element_type=jnp.float32
        )
        return (carry + update, None)

    initial = jnp.zeros((row_block.shape[0], queries.shape[2]), jnp.float32)
    inputs = (
        step_view(queries, slot_count),
        step_view(targets, slot_count),
        step_view(slot_norms, slot_count),
        step_view(active, slot_count),
    )
    result, unused = lax.scan(one_step, initial, inputs)
    return result


def per_device(
    entities,
    relations,
    candidate_blocks,
    list_lengths,
    head_offsets,
    relation_offsets,
    target_codes,
):
    entity_count = lax.axis_size("entity")
    owner = lax.axis_index("entity")
    table = entities[0]
    block_rows = table.shape[0]
    local_relations = relations.shape[0]
    head_rows = jnp.take(table, head_offsets, axis=0)
    products = jnp.einsum("td,rde->tre", head_rows, relations, precision=lax.Precision.HIGHEST)
    selector = (
        relation_offsets[:, None] == jnp.arange(local_relations, dtype=jnp.int32)[None, :]
    ).astype(jnp.float32)
    query = jnp.sum(products * selector[:, :, None], axis=1).astype(jnp.bfloat16)
    gathered, all_codes = (
        lax.all_gather(query[None], "entity", axis=0, tiled=True),
        lax.all_gather(target_codes[None], "entity", axis=0, tiled=True),
    )
    lengths = list_lengths[0]
    entry_index = jnp.arange(candidate_blocks.shape[1], dtype=jnp.int32)
    counted = entry_index[None, :] < lengths[:, None]
    listed = jnp.any(counted & (candidate_blocks == owner), axis=1)
    ranking = jnp.cumsum(listed.astype(jnp.int32)) - 1
    capacity = min(CAP, entity_count)
    slot_index = jnp.arange(capacity, dtype=jnp.int32)
    set_numbers = jnp.arange(entity_count, dtype=jnp.int32)
    matches = listed[None, :] & (ranking[None, :] == slot_index[:, None])
    slot_set = jnp.sum(jnp.where(matches, set_numbers[None, :], 0), axis=1)
    slot_used = jnp.any(matches, axis=1)
    slot_queries = jnp.take(gathered, slot_set, axis=0)
    slot_codes = jnp.take(all_codes, slot_set, axis=0)
    slot_lists = jnp.take(candidate_blocks, slot_set, axis=0)
    slot_lengths = jnp.take(lengths, slot_set)
    chosen = slot_codes // block_rows % slot_lengths[:, None]
    target_block = jnp.sum(
        jnp.where(chosen[:, :, None] == entry_index[None, None, :], slot_lists[:, None, :], 0),
        axis=2,
    )
    slot_targets = jnp.where(target_block == owner, slot_codes % block_rows, -1)
    rounded_table = table.astype(jnp.bfloat16)
    maxima, masses, picked = slot_stats(rounded_table, slot_queries, slot_targets, slot_used)
    safe_rank = jnp.clip(ranking, 0, capacity - 1)
    set_max = jnp.where(listed[:, None], jnp.take(maxima, safe_rank, axis=0), negative_floor)
    set_mass = jnp.where(listed[:, None], jnp.take(masses, safe_rank, axis=0), 0.0)
    set_target = jnp.where(listed[:, None], jnp.take(picked, safe_rank, axis=0), 0.0)
    top_max = lax.pmax(set_max.astype(jnp.bfloat16), "entity").astype(set_max.dtype)
    scaled_mass = set_mass * jnp.exp(set_max - top_max)
    top_mass, top_target = lax.psum((scaled_mass, set_target), "entity")
    log_norm = top_max + jnp.log(top_mass)
    loss = lax.dynamic_index_in_dim(log_norm - top_target, owner, 0, keepdims=False)
    slot_norms = jnp.take(log_norm, slot_set, axis=0)
    gradient = lax.psum_scatter(
        slot_grads(rounded_table, slot_queries, slot_targets, slot_used, slot_norms),
        "dp",
        scatter_dimension=0,
        tiled=True,
    )
    return (loss, gradient[None])


LOADS = 4
META = 16
LAG = 2
PAIRS = 16
TILE = 256


def split3(value):
    first = value.astype(jnp.bfloat16)
    rest = value - first.astype(jnp.float32)
    second = rest.astype(jnp.bfloat16)
    third = (rest - second.astype(jnp.float32)).astype(jnp.bfloat16)
    return first, second, third


def fused_kernel(
    lists_ref,
    lengths_ref,
    heads_ref,
    kinds_ref,
    codes_ref,
    table_hbm,
    relations_hbm,
    loss_ref,
    grad_ref,
    table,
    operators,
    keys,
    head_rows,
    kind_rows,
    product,
    chunks,
    masses,
    maxima,
    stats,
    from_sibling,
    from_z,
    from_plane,
    load_sem,
    z_send,
    z_recv,
    x_send,
    x_recv,
    y_send,
    y_recv,
    xd_send,
    xd_recv,
    yd_send,
    yd_recv,
    s_send,
    s_recv,
    stat_send,
    stat_recv,
):
    a = lax.axis_index("dp")
    e = lax.axis_index("entity")
    z, c = e // 2, e % 2
    block_rows, width = table.shape
    share = keys.shape[0]
    trips = codes_ref.shape[1]
    chunk_rows = trips + META
    first_rows = 80
    kinds = operators.shape[0]

    def group(g):
        return ((a // 2 + g // 2) % 2) * 2 + (a % 2 + g % 2) % 2

    def chunk_of(g, j, core):
        return group(g) * 8 + ((z + 4 - j) % 4) * 2 + core

    sibling = (a, z * 2 + 1 - c)
    plane = [(group(g), e) for g in (1, 2, 3)]
    along_z = [(a, ((z + j) % 4) * 2 + c) for j in (1, 2, 3)]
    x_device, y_device = plane[0], plane[1]

    def remote(source, target, send_sem, recv_sem, device):
        return pltpu.make_async_remote_copy(
            src_ref=source,
            dst_ref=target,
            send_sem=send_sem,
            recv_sem=recv_sem,
            device_id=device,
            device_id_type=pl.DeviceIdType.MESH,
        )

    barrier = pltpu.get_barrier_semaphore()
    for device in [sibling] + plane + along_z:
        pl.semaphore_signal(barrier, inc=1, device_id=device, device_id_type=pl.DeviceIdType.MESH)

    table_load = pltpu.make_async_copy(table_hbm.at[0], table, load_sem.at[LOADS])
    table_load.start()
    per_load = kinds // LOADS
    loads = []
    for n in range(LOADS):
        span = pl.ds(n * per_load, per_load)
        load = pltpu.make_async_copy(relations_hbm.at[span], operators.at[span], load_sem.at[n])
        load.start()
        loads.append(load)

    length = lengths_ref[0, e]
    codes = codes_ref[...]
    entry = codes // block_rows
    wraps = jnp.zeros_like(entry)
    for n in range(1, 4):
        wraps = wraps + jnp.where(entry >= n * length, 1, 0)
    pick = entry - wraps * length
    row_index = lax.broadcasted_iota(jnp.int32, (META, trips), 0)
    target_block = jnp.zeros_like(entry)
    used = jnp.zeros((META, trips), jnp.float32)
    for k in range(lists_ref.shape[1]):
        named = lists_ref[e, k]
        target_block = target_block + jnp.where(pick == k, named, 0)
        counted = jnp.where(k < length, named, -9)
        used = used + jnp.where(row_index - 2 == counted, 1.0, 0.0)
    target_id = target_block * block_rows + codes % block_rows
    high = (target_id // 256).astype(jnp.float32)
    low = (target_id % 256).astype(jnp.float32)
    notes = jnp.where(row_index == 0, high, jnp.where(row_index == 1, low, used))

    table_load.wait()

    def fetch(n, unused):
        head_rows[pl.ds(n, 1), :] = table[pl.ds(heads_ref[n], 1), :]
        kind_rows[pl.ds(n, 1), :] = jnp.full((1, width), kinds_ref[n], jnp.int32)
        return unused

    lax.fori_loop(0, trips, fetch, 0, unroll=8)
    parts = jnp.concatenate(split3(head_rows[...]), axis=0)

    def one_kind(r, unused):
        r1, r2, r3 = split3(operators[r])
        p1 = jnp.dot(parts, r1, preferred_element_type=jnp.float32)
        p2 = jnp.dot(parts[: 2 * trips], r2, preferred_element_type=jnp.float32)
        p3 = jnp.dot(parts[:trips], r3, preferred_element_type=jnp.float32)
        small = (p1[2 * trips :] + p2[trips:]) + p3
        total = p1[:trips] + ((p1[trips : 2 * trips] + p2[:trips]) + small)
        product[...] = jnp.where(kind_rows[...] == r, total, product[...])
        return unused

    product[...] = jnp.zeros_like(product)
    for n in range(LOADS):
        loads[n].wait()
        lax.fori_loop(n * per_load, (n + 1) * per_load, one_kind, 0, unroll=2)

    mine = chunk_of(0, 0, c)
    chunks[mine, 0:trips, :] = product[...].astype(jnp.bfloat16)
    chunks[mine, trips:chunk_rows, :] = jnp.concatenate(
        [notes, jnp.zeros_like(notes)], axis=1
    ).astype(jnp.bfloat16)

    pl.semaphore_wait(barrier, 7)

    def z_copy(j, slot):
        return remote(
            chunks.at[slot], chunks.at[slot], z_send.at[j - 1], z_recv.at[j - 1], along_z[j - 1]
        )

    for j in (1, 2, 3):
        z_copy(j, mine).start()

    keys[...] = table[pl.ds(pl.multiple_of(a * share, share), share), :].astype(jnp.bfloat16)

    def x_copy(j, slot):
        return remote(chunks.at[slot], chunks.at[slot], x_send.at[j], x_recv.at[j], x_device)

    def y_copy(j, slot):
        return remote(chunks.at[slot], chunks.at[slot], y_send.at[j], y_recv.at[j], y_device)

    def yd_copy(j, slot):
        part = chunks.at[slot, pl.ds(0, first_rows)]
        return remote(part, part, yd_send.at[j], yd_recv.at[j], y_device)

    def xd_copy(j, slot):
        part = chunks.at[slot, pl.ds(first_rows, chunk_rows - first_rows)]
        return remote(part, part, xd_send.at[j], xd_recv.at[j], x_device)

    def s_copy(i, slot):
        return remote(chunks.at[slot], chunks.at[slot], s_send.at[i], s_recv.at[i], sibling)

    def pair_of(i):
        return group(i % 4) * 4 + (z + 4 - i // 4) % 4

    def read_notes(pair):
        sheet = jnp.concatenate(
            [chunks[pair * 2 + n, trips:chunk_rows, 0:trips] for n in range(2)], axis=1
        ).astype(jnp.float32)
        rows = lax.broadcasted_iota(jnp.int32, sheet.shape, 0)
        in_use = jnp.sum(jnp.where(rows == 2 + e, sheet, 0.0), axis=0, keepdims=True) > 0.0
        target = (sheet[0:1] * 256.0 + sheet[1:2]).astype(jnp.int32)
        return in_use, target - (e * block_rows + a * share)

    def pair_queries(pair):
        return jnp.concatenate([chunks[pair * 2 + n, 0:trips, :] for n in range(2)], axis=0)

    row_iota = lax.broadcasted_iota(jnp.int32, (TILE, 2 * trips), 0)

    def fold(value, op):
        return op(value.reshape(TILE // 8, 8, 2 * trips), axis=0)

    def pair_stats(pair):
        queries = pair_queries(pair)
        in_use, target = read_notes(pair)
        top = None
        for n in range(share // TILE):
            scores = lax.dot_general(
                keys[n * TILE : (n + 1) * TILE, :],
                queries,
                (((1,), (1,)), ((), ())),
                preferred_element_type=jnp.float32,
            )
            masses[pair, n * TILE : (n + 1) * TILE, :] = scores
            tile_top = fold(scores, jnp.max)
            top = tile_top if top is None else jnp.maximum(top, tile_top)
        top = jnp.max(top, axis=0, keepdims=True)
        total = jnp.zeros((8, 2 * trips), jnp.float32)
        picked = jnp.zeros((8, 2 * trips), jnp.float32)
        for n in range(share // TILE):
            scores = masses[pair, n * TILE : (n + 1) * TILE, :]
            mass = jnp.exp(scores - top)
            masses[pair, n * TILE : (n + 1) * TILE, :] = mass
            total = total + fold(mass, jnp.sum)
            picked = picked + fold(jnp.where(row_iota == target - n * TILE, scores, 0.0), jnp.sum)
        total = jnp.sum(total, axis=0, keepdims=True)
        maxima[pl.ds(pair, 1), :] = top
        stats[0, 0, pl.ds(pair, 1), :] = jnp.where(in_use, top + jnp.log(total), negative_floor)
        stats[0, 1, pl.ds(pair, 1), :] = jnp.sum(picked, axis=0, keepdims=True)

    def gather_step(i, unused):
        j, g = i // 4, i % 4

        @pl.when(i < PAIRS)
        def _():
            slot = chunk_of(g, j, c)

            @pl.when(g == 0)
            def _():
                for k in (1, 2, 3):

                    @pl.when(j == k)
                    def _():
                        z_copy(k, slot).wait_recv()

                x_copy(j, slot).start()
                y_copy(j, slot).start()

            @pl.when(g == 1)
            def _():
                x_copy(j, slot).wait_recv()
                yd_copy(j, slot).start()

            @pl.when(g == 2)
            def _():
                y_copy(j, slot).wait_recv()
                xd_copy(j, slot).start()

            @pl.when(g == 3)
            def _():
                yd_copy(j, slot).wait_recv()
                xd_copy(j, slot).wait_recv()

            s_copy(i, slot).start()

        @pl.when(i >= LAG)
        def _():
            k = i - LAG
            s_copy(k, chunk_of(k % 4, k // 4, 1 - c)).wait_recv()
            pair_stats(pair_of(k))

        return unused

    lax.fori_loop(0, PAIRS + LAG, gather_step, 0)

    def merge(sheets):
        top = sheets[0][0]
        for sheet in sheets[1:]:
            top = jnp.maximum(top, sheet[0])
        total = sum(jnp.exp(sheet[0] - top) for sheet in sheets)
        return top + jnp.log(total), sum(sheet[1] for sheet in sheets)

    def exchange(level, targets, devices, first):
        copies = []
        for n, (target, device) in enumerate(zip(targets, devices)):
            copy = remote(
                stats.at[level], target, stat_send.at[first + n], stat_recv.at[first + n], device
            )
            copy.start()
            copies.append(copy)
        for copy in copies:
            copy.wait()
        return merge([stats[level]] + [target[...] for target in targets])

    norm, hit = exchange(0, [from_sibling], [sibling], 0)
    stats[1, 0], stats[1, 1] = norm, hit
    norm, hit = exchange(1, [from_z.at[n] for n in range(3)], along_z, 1)
    stats[2, 0], stats[2, 1] = norm, hit
    norm, hit = exchange(2, [from_plane.at[n] for n in range(3)], plane, 4)
    stats[3, 0], stats[3, 1] = norm, norm - hit

    own = stats[3, 1, pl.ds(a * 4 + z, 1), :]
    loss_ref[...] = jnp.where(c == 0, own[:, :trips], own[:, trips:])

    grad_ref[...] = jnp.zeros_like(grad_ref)

    def gradient_step(quad, unused):
        scales, targets = [], []
        for n in range(4):
            pair = quad * 4 + n
            in_use, target = read_notes(pair)
            gap = maxima[pl.ds(pair, 1), :] - stats[3, 0, pl.ds(pair, 1), :]
            scales.append(jnp.where(in_use, jnp.exp(gap), 0.0))
            targets.append(target)
        queries = jnp.concatenate([pair_queries(quad * 4 + n) for n in range(4)], axis=0)
        for m in range(share // TILE):
            coefficients = jnp.concatenate(
                [
                    (
                        masses[quad * 4 + n, m * TILE : (m + 1) * TILE, :] * scales[n]
                        - jnp.where(row_iota == targets[n] - m * TILE, 1.0, 0.0)
                    ).astype(jnp.bfloat16)
                    for n in range(4)
                ],
                axis=1,
            )
            grad_ref[m * TILE : (m + 1) * TILE, :] += jnp.dot(
                coefficients, queries, preferred_element_type=jnp.float32
            )
        return unused

    lax.fori_loop(0, PAIRS // 4, gradient_step, 0)

    def drain(i, unused):
        s_copy(i, chunk_of(i % 4, i // 4, c)).wait_send()
        return unused

    lax.fori_loop(0, PAIRS, drain, 0)
    for j in range(4):
        if j > 0:
            z_copy(j, mine).wait_send()
        x_copy(j, chunk_of(0, j, c)).wait_send()
        y_copy(j, chunk_of(0, j, c)).wait_send()
        yd_copy(j, chunk_of(1, j, c)).wait_send()
        xd_copy(j, chunk_of(2, j, c)).wait_send()


def fused_device(
    entities,
    relations,
    candidate_blocks,
    list_lengths,
    head_offsets,
    relation_offsets,
    target_codes,
):
    block_rows, width = entities.shape[1:]
    trips = target_codes.shape[0]
    share = block_rows // 4
    dma = pltpu.SemaphoreType.DMA
    smem = pl.BlockSpec(memory_space=pltpu.SMEM)
    vmem = pl.BlockSpec(memory_space=pltpu.VMEM)
    anywhere = pl.BlockSpec(memory_space=pl.ANY)
    sheet = (2, PAIRS, 2 * trips)
    loss, gradient = pl.pallas_call(
        fused_kernel,
        out_shape=(
            jax.ShapeDtypeStruct((1, trips), jnp.float32),
            jax.ShapeDtypeStruct((share, width), jnp.float32),
        ),
        in_specs=[smem, smem, smem, smem, vmem, anywhere, anywhere],
        out_specs=(vmem, vmem),
        scratch_shapes=[
            pltpu.VMEM((block_rows, width), jnp.float32),
            pltpu.VMEM(relations.shape, jnp.float32),
            pltpu.VMEM((share, width), jnp.bfloat16),
            pltpu.VMEM((trips, width), jnp.float32),
            pltpu.VMEM((trips, width), jnp.int32),
            pltpu.VMEM((trips, width), jnp.float32),
            pltpu.VMEM((2 * PAIRS, trips + META, width), jnp.bfloat16),
            pltpu.VMEM((PAIRS, share, 2 * trips), jnp.float32),
            pltpu.VMEM((PAIRS, 2 * trips), jnp.float32),
            pltpu.VMEM((4,) + sheet, jnp.float32),
            pltpu.VMEM(sheet, jnp.float32),
            pltpu.VMEM((3,) + sheet, jnp.float32),
            pltpu.VMEM((3,) + sheet, jnp.float32),
            dma((LOADS + 1,)),
            dma((3,)),
            dma((3,)),
            dma((4,)),
            dma((4,)),
            dma((4,)),
            dma((4,)),
            dma((4,)),
            dma((4,)),
            dma((4,)),
            dma((4,)),
            dma((PAIRS,)),
            dma((PAIRS,)),
            dma((7,)),
            dma((7,)),
        ],
        compiler_params=pltpu.CompilerParams(
            collective_id=0, has_side_effects=True, vmem_limit_bytes=56 * 1024 * 1024
        ),
        name="rescal_step",
    )(
        candidate_blocks,
        list_lengths,
        head_offsets,
        relation_offsets,
        target_codes[None],
        entities,
        relations,
    )
    return (loss.reshape(trips), gradient[None])


def solution(mesh):
    small = mesh.shape["dp"] == 4 and mesh.shape["entity"] == 8
    return jax.shard_map(
        fused_device if small else per_device,
        mesh=mesh,
        in_specs=(
            P("entity", None, None),
            P("entity", None, None),
            P("dp", None),
            P("dp", None),
            P(("dp", "entity")),
            P(("dp", "entity")),
            P(("dp", "entity")),
        ),
        out_specs=(P(("dp", "entity")), P("entity", "dp", None)),
        check_vma=False,
    )
```
